256 devices in a mesh: row: 16 (over z_lo, y, core), col: 16 (over z_hi, x).
Axes of the slice: x: 4, y: 4, z: 8 (z_hi: 4, z_lo: 2; z = z_hi * 2 + z_lo), core: 2. Of those that a mesh axis runs over, the one named last changes fastest.
Arguments:
- latent: float32 [256, 5280], P('row', 'col'), may hold values from -6 to 6
- embedded: float32 [256, 5280], P('row', 'col'), may hold values from -6 to 6
- cotangent: float32 [256, 5280], P('row', 'col'), may hold values from -6 to 6
- gain: float32 [5280], P('col'), may hold values from 0.25 to 1.75
- gate_weight: bfloat16 [5280, 17920], P('col', 'row'), may hold values from -0.078125 to 0.078125
- up_weight: bfloat16 [5280, 17920], P('col', 'row'), may hold values from -0.078125 to 0.078125
- down_weight: bfloat16 [17920, 5280], P('row', 'col'), may hold values from -0.046875 to 0.046875
- gate_sign: int32 [5280, 17920], P('col', 'row'), may hold values from 0 to 1
- up_sign: int32 [5280, 17920], P('col', 'row'), may hold values from 0 to 1
- down_sign: int32 [17920, 5280], P('row', 'col'), may hold values from 0 to 1
Outputs:
- gate_estimate: float32 [5280, 17920], P('col', 'row')
- up_estimate: float32 [5280, 17920], P('col', 'row')
- down_estimate: float32 [17920, 5280], P('row', 'col')
The draws below stay inside these ranges and needn't reach their ends.
All inputs are finite; a program needn't handle non-finite values.
Results may differ from the reference program's by a relative error of at most 0.034.
Values may be sent and summed in bfloat16 or wider, within the bound.
No kernel may reach another device: no remote copies, remote signals or barrier semaphores. Data moves between devices by JAX's collectives and lax.ppermute only.
A program may use at most 128 MiB of HBM per device.

```python
import jax
import jax.numpy as jnp
from jax import lax

D = 5280
FF = 17920
ITERS = 2
TOKENS = 256
N_COL = 16


def set_ends(array, key, low, largest):
    extent = array.shape
    index_at = [jax.random.randint(jax.random.fold_in(key, axis), (), 0, extent[axis]) for axis in range(len(extent))]
    array = array.at[tuple(index_at)].set(low)
    longest = extent.index(max(extent))
    index_at[longest] = (index_at[longest] + 1) % extent[longest]
    return array.at[tuple(index_at)].set(largest)


def block_scale(stream_key, extent, cuts, smallest, largest):
    def one(dim, blocks):
        heights = jax.random.uniform(jax.random.fold_in(jax.random.fold_in(stream_key, 6), dim), (blocks,), jnp.float32, smallest / len(cuts), largest / len(cuts))
        return jnp.repeat(jnp.exp(heights), extent[dim] // blocks).reshape((-1,) + (1,) * (len(extent) - dim - 1))

    loudness = one(*cuts[0])
    for cut in cuts[1:]:
        loudness = loudness * one(*cut)
    return loudness


def centred(own_key, extent, scale, limit, shards=(), held_as=jnp.bfloat16):
    drawn = jax.random.normal(own_key, extent, jnp.float32) * scale
    if len(shards) > 0:
        drawn = block_scale(own_key, extent, shards, -0.22, 0.18) * drawn
    return jnp.clip(drawn, min=-limit, max=limit).astype(held_as)


def setup_inputs(seed: int = 0) -> dict:
    splits = jax.random.split(jax.random.key(seed), 11)
    latent = centred(splits[0], (TOKENS, D), 1.0, 6.0, ((0, 16), (1, 16)), jnp.float32)
    embedded = centred(splits[1], (TOKENS, D), 1.0, 6.0, ((0, 16), (1, 16)), jnp.float32)
    cotangent = centred(splits[2], (TOKENS, D), 1.0, 6.0, ((0, 16), (1, 16)), jnp.float32)
    gain = jnp.clip(1.0 + 0.15 * jax.random.normal(splits[3], (D,), jnp.float32), 0.25, 1.75)
    gate_weight = centred(splits[4], (D, FF), D ** -0.5, 0.078125, ((0, 16), (1, 16)))
    up_weight = centred(splits[5], (D, FF), D ** -0.5, 0.078125, ((0, 16), (1, 16)))
    down_weight = centred(splits[6], (FF, D), FF ** -0.5, 0.046875, ((0, 16), (1, 16)))
    gate_sign = set_ends(jax.random.randint(splits[7], (D, FF), 0, 2), jax.random.fold_in(splits[7], 1), 0, 1).astype(jnp.int32)
    up_sign = set_ends(jax.random.randint(splits[8], (D, FF), 0, 2), jax.random.fold_in(splits[8], 1), 0, 1).astype(jnp.int32)
    down_sign = set_ends(jax.random.randint(splits[9], (FF, D), 0, 2), jax.random.fold_in(splits[9], 1), 0, 1).astype(jnp.int32)
    return dict(latent=latent, embedded=embedded, cotangent=cotangent, gain=gain, gate_weight=gate_weight, up_weight=up_weight, down_weight=down_weight, gate_sign=gate_sign, up_sign=up_sign, down_sign=down_sign)


EPS = 1e-06

def hidden_forward(pg, pu, t_pg, t_pu):
    sg = jax.nn.sigmoid(pg)
    act = pg * sg
    slope = sg * (1.0 + pg * (1.0 - sg))
    hidden = act * pu
    t_hidden = slope * t_pg * pu + act * t_pu
    return (hidden.astype(jnp.bfloat16), t_hidden.astype(jnp.bfloat16))

def hidden_backward(pg, pu, t_pg, t_pu, c_h, t_c_h):
    sg = jax.nn.sigmoid(pg)
    act = pg * sg
    slope = sg * (1.0 + pg * (1.0 - sg))
    curve = sg * (1.0 - sg) * (2.0 + pg * (1.0 - 2.0 * sg))
    c_pg = c_h * pu * slope
    c_pu = c_h * act
    t_c_pg = t_c_h * pu * slope + c_h * t_pu * slope + c_h * pu * curve * t_pg
    t_c_pu = t_c_h * act + c_h * slope * t_pg
    bf = jnp.bfloat16
    return (c_pg.astype(bf), c_pu.astype(bf), t_c_pg.astype(bf), t_c_pu.astype(bf))

def norm_backward(a_val, r_val, t_a, t_r, gain, c_x, t_c_x, p_val, t_p):
    q_val = gain * c_x
    t_q = gain * t_c_x
    r_cube = r_val * r_val * r_val
    c_a = r_val * q_val - r_cube * p_val * a_val
    t_c_a = t_r * q_val + r_val * t_q - 3.0 * r_val * r_val * t_r * p_val * a_val - r_cube * t_p * a_val - r_cube * p_val * t_a
    return (c_a, t_c_a)

def direction(sign, fan_in):
    return ((2 * sign - 1).astype(jnp.float32) * float(fan_in) ** (-0.5)).astype(jnp.bfloat16)

def mdot(left, right):
    return jnp.dot(left, right, preferred_element_type=jnp.float32)

def block_sum(pairs):
    width = pairs[0][0].shape[1] // N_COL
    total = None
    for block in range(N_COL):
        low = block * width
        part = None
        for left, right in pairs:
            term = mdot(left[:, low:low + width], right[low:low + width, :])
            part = term if part is None else part + term
        rounded = lax.optimization_barrier(part.astype(jnp.bfloat16)).astype(jnp.float32)
        total = rounded if total is None else total + rounded
    return total

def reference(latent, embedded, cotangent, gain, gate_weight, up_weight, down_weight, gate_sign, up_sign, down_sign):
    dir_gate = direction(gate_sign, D)
    dir_up = direction(up_sign, D)
    dir_down = direction(down_sign, FF)
    state = latent
    t_state = jnp.zeros_like(latent)
    saved = []
    for step in range(ITERS):
        a_val = state + embedded
        t_a = t_state
        sum_sq = lax.optimization_barrier(jnp.sum(a_val * a_val, axis=-1, keepdims=True))
        sum_tan = lax.optimization_barrier(jnp.sum(a_val * t_a, axis=-1, keepdims=True))
        r_val = lax.rsqrt(sum_sq / D + EPS)
        t_r = -0.5 * r_val * r_val * r_val * (2.0 * sum_tan / D)
        x_b = (a_val * r_val * gain).astype(jnp.bfloat16)
        t_x = ((t_a * r_val + a_val * t_r) * gain).astype(jnp.bfloat16)
        pg = block_sum([(x_b, gate_weight)])
        pu = block_sum([(x_b, up_weight)])
        t_pg = block_sum([(t_x, gate_weight), (x_b, dir_gate)])
        t_pu = block_sum([(t_x, up_weight), (x_b, dir_up)])
        h_b, t_h = hidden_forward(pg, pu, t_pg, t_pu)
        y_val = mdot(h_b, down_weight)
        t_y = mdot(t_h, down_weight) + mdot(h_b, dir_down)
        saved.append((a_val, t_a, r_val, t_r, x_b, t_x, pg, pu, t_pg, t_pu, h_b, t_h))
        state = state + y_val
        t_state = t_state + t_y
    c_state = cotangent
    t_c_state = jnp.zeros_like(cotangent)
    acc_gate = jnp.zeros(gate_weight.shape, jnp.float32)
    acc_up = jnp.zeros(up_weight.shape, jnp.float32)
    acc_down = jnp.zeros(down_weight.shape, jnp.float32)
    down_t = down_weight.T
    dir_down_t = dir_down.T
    for step in reversed(range(ITERS)):
        a_val, t_a, r_val, t_r, x_b, t_x, pg, pu, t_pg, t_pu, h_b, t_h = saved[step]
        c_y = c_state.astype(jnp.bfloat16)
        t_c_y = t_c_state.astype(jnp.bfloat16)
        acc_down = acc_down + mdot(t_h.T, c_y) + mdot(h_b.T, t_c_y)
        c_h = block_sum([(c_y, down_t)])
        t_c_h = block_sum([(t_c_y, down_t), (c_y, dir_down_t)])
        c_pg, c_pu, t_c_pg, t_c_pu = hidden_backward(pg, pu, t_pg, t_pu, c_h, t_c_h)
        acc_gate = acc_gate + mdot(t_x.T, c_pg) + mdot(x_b.T, t_c_pg)
        acc_up = acc_up + mdot(t_x.T, c_pu) + mdot(x_b.T, t_c_pu)
        c_x = mdot(c_pg, gate_weight.T) + mdot(c_pu, up_weight.T)
        t_c_x = mdot(t_c_pg, gate_weight.T) + mdot(c_pg, dir_gate.T) + mdot(t_c_pu, up_weight.T) + mdot(c_pu, dir_up.T)
        q_val = gain * c_x
        t_q = gain * t_c_x
        p_val = lax.optimization_barrier(jnp.sum(a_val * q_val, axis=-1, keepdims=True)) / D
        t_p = lax.optimization_barrier(jnp.sum(t_a * q_val + a_val * t_q, axis=-1, keepdims=True)) / D
        c_a, t_c_a = norm_backward(a_val, r_val, t_a, t_r, gain, c_x, t_c_x, p_val, t_p)
        c_state = c_state + c_a
        t_c_state = t_c_state + t_c_a
    gate_est = (2 * gate_sign - 1).astype(jnp.float32) * acc_gate
    up_est = (2 * up_sign - 1).astype(jnp.float32) * acc_up
    down_est = (2 * down_sign - 1).astype(jnp.float32) * acc_down
    return (gate_est, up_est, down_est)
```

```python
import jax
import jax.numpy as jnp
from jax import lax
from jax.sharding import PartitionSpec as P

D = 5280
FF = 17920
ITERS = 2
EPS = 1e-06

FEAT = 330
WIDE = 384
HID = 1120
SPAN = 1152
BF = jnp.bfloat16
F32 = jnp.float32

AT_X = [[(z * 4 + x, z * 4 + (x + k) % 4) for z in range(4) for x in range(4)] for k in range(4)]
AT_Z = [[(z * 4 + x, (z + k) % 4 * 4 + x) for z in range(4) for x in range(4)] for k in range(4)]
ALONG_X = [[z * 4 + x for x in range(4)] for z in range(4)]
ALONG_Z = [[z * 4 + x for z in range(4)] for x in range(4)]


def mdot(left, right):
    return jnp.dot(left, right, preferred_element_type=F32)


def inner_rows(left, right):
    return lax.dot_general(left, right, (((0,), (0,)), ((), ())), preferred_element_type=F32)


def inner_cols(left, right):
    return lax.dot_general(left, right, (((1,), (1,)), ((), ())), preferred_element_type=F32)


def direction(sign, fan_in):
    return ((2 * sign - 1).astype(F32) * float(fan_in) ** (-0.5)).astype(BF)


def pad_to(array, rows, columns):
    return jnp.pad(array, ((0, rows - array.shape[0]), (0, columns - array.shape[1])))


def side_by_side(first, second):
    return jnp.concatenate([pad_to(first, WIDE, SPAN), pad_to(second, WIDE, SPAN)], axis=1)


def split_two(total):
    high = total.astype(BF)
    return high, (total - high.astype(F32)).astype(BF)


def exchange_sum(chunks, axis, place, perms):
    pieces = lax.optimization_barrier(
        tuple(lax.dynamic_index_in_dim(chunks, (place + k) % 4, axis, keepdims=False) for k in range(4))
    )
    got = lax.optimization_barrier(tuple(lax.ppermute(pieces[k], "col", perms[k]) for k in range(1, 4)))
    total = pieces[0].astype(F32)
    for piece in got:
        total = total + piece.astype(F32)
    return total


def reduce_x(partial, x, stats):
    width = partial.shape[1]
    total = exchange_sum(partial.astype(BF).reshape(4, 4, 16, width), 1, x, AT_X).reshape(64, width)
    if stats:
        lane = lax.broadcasted_iota(jnp.int32, (64, width), 1)
        for at in (HID, HID + 2):
            high, low = split_two(total[:, at : at + 1] + total[:, at + 1 : at + 2])
            total = jnp.where(lane == at, high.astype(F32), total)
            total = jnp.where(lane == at + 1, low.astype(F32), total)
    return total.astype(BF).reshape(4, 16, width)


def reduce_z(partial, z):
    return exchange_sum(partial, 0, z, AT_Z)


def reduce_hidden(first, second, x, z, stats=False):
    first = reduce_x(first, x, stats)
    second = reduce_x(second, x, False)
    return reduce_z(first, z), reduce_z(second, z)


def reduce_hidden_aside(partial):
    half = lax.psum_scatter(
        partial.astype(BF).reshape(4, 4, 16, -1), "col", scatter_dimension=1, axis_index_groups=ALONG_X, tiled=True
    )
    return lax.psum_scatter(
        half.reshape(64, -1), "col", scatter_dimension=0, axis_index_groups=ALONG_Z, tiled=True
    ).astype(F32)


def gather_z(block, z):
    got = lax.optimization_barrier(tuple(lax.ppermute(block, "col", AT_Z[k]) for k in range(1, 4)))
    out = jnp.zeros((4, 1) + block.shape, block.dtype)
    for k, piece in enumerate((block,) + got):
        out = lax.dynamic_update_slice_in_dim(out, piece[None, None], (z - k) % 4, 0)
    return out


def gather_x(block, x):
    got = lax.optimization_barrier(tuple(lax.ppermute(block, "col", AT_X[k]) for k in range(1, 4)))
    out = jnp.zeros((4, 4) + block.shape[2:], block.dtype)
    for k, piece in enumerate((block,) + got):
        out = lax.dynamic_update_slice_in_dim(out, piece, (x - k) % 4, 1)
    return out.reshape(256, -1)


def gather_hidden(first, second, x, z):
    first = gather_z(first, z)
    second = gather_z(second, z)
    return gather_x(first, x), gather_x(second, x)


def sum_col(tiny):
    for perms in (AT_Z, AT_X):
        got = lax.optimization_barrier(tuple(lax.ppermute(tiny, "col", perms[k]) for k in range(1, 4)))
        tiny = tiny + got[0] + got[1] + got[2]
    return tiny


def after(array, other):
    return array + (0.0 * other[:1, :1].astype(F32)).astype(array.dtype)


def reduce_features(first, second):
    partial = jnp.concatenate([first, second], axis=1).astype(BF).reshape(16, 16, 2 * WIDE)
    got = lax.all_to_all(partial, "row", 0, 0)
    total = jnp.sum(got.astype(F32), axis=0)
    return total[:, :FEAT], total[:, WIDE : WIDE + FEAT]


def token_block(first, second, stats=None):
    if stats is None:
        spare = jnp.zeros((16, 4), BF)
    else:
        spare = jnp.concatenate(split_two(stats[0]) + split_two(stats[1]), axis=1)
    return jnp.concatenate(
        [first.astype(BF), spare, jnp.zeros((16, WIDE - FEAT - 4), BF), second.astype(BF), jnp.zeros((16, WIDE - FEAT), BF)], axis=1
    )


def gather_tokens(block):
    full = lax.all_gather(block, "row", axis=0, tiled=True)
    return tuple(full[:, at : at + WIDE] for at in range(0, full.shape[1], WIDE))


def halves(array):
    return array[:, :HID], array[:, SPAN : SPAN + HID]


def joined(first, second):
    return jnp.concatenate([pad_to(first.astype(BF), 16, SPAN), pad_to(second.astype(BF), 16, SPAN)], axis=1)


def hidden_forward(pg, pu, t_pg, t_pu):
    sg = jax.nn.sigmoid(pg)
    act = pg * sg
    slope = sg * (1.0 + pg * (1.0 - sg))
    return act * pu, slope * t_pg * pu + act * t_pu


def hidden_backward(pg, pu, t_pg, t_pu, c_h, t_c_h):
    sg = jax.nn.sigmoid(pg)
    act = pg * sg
    slope = sg * (1.0 + pg * (1.0 - sg))
    curve = sg * (1.0 - sg) * (2.0 + pg * (1.0 - 2.0 * sg))
    c_pg = c_h * pu * slope
    c_pu = c_h * act
    t_c_pg = t_c_h * pu * slope + c_h * t_pu * slope + c_h * pu * curve * t_pg
    t_c_pu = t_c_h * act + c_h * slope * t_pg
    return c_pg, c_pu, t_c_pg, t_c_pu


def row_sum(array):
    return jnp.sum(array, axis=-1, keepdims=True)


def per_device(
    latent,
    embedded,
    cotangent,
    gain,
    gate_weight,
    up_weight,
    down_weight,
    gate_sign,
    up_sign,
    down_sign,
):
    place = lax.axis_index("col")
    x = place % 4
    z = place // 4
    weights = side_by_side(gate_weight, up_weight)
    row = lax.broadcasted_iota(jnp.int32, (WIDE, 2 * SPAN), 0)
    column = lax.broadcasted_iota(jnp.int32, (WIDE, 2 * SPAN), 1)
    passes = (row >= FEAT) & (row < FEAT + 4) & (column - HID == row - FEAT)
    weights_in = jnp.where(passes, jnp.ones((), BF), weights)
    dirs = side_by_side(direction(gate_sign, D), direction(up_sign, D))
    down = pad_to(down_weight.T, WIDE, SPAN)
    dir_down = pad_to(direction(down_sign.T, FF), WIDE, SPAN)

    state = latent
    t_state = jnp.zeros_like(latent)
    c_state = cotangent
    t_c_state = jnp.zeros_like(cotangent)
    saved = []
    for step in range(ITERS):
        a_val = state + embedded
        t_a = t_state
        stats = (row_sum(a_val * a_val), row_sum(a_val * t_a))
        block = token_block(a_val * gain, t_a * gain, stats)
        if step == 0:
            u_full, v_full, c_y, t_c_y = gather_tokens(
                jnp.concatenate([block, token_block(c_state, t_c_state)], axis=1)
            )
        else:
            u_full, v_full = gather_tokens(block)
        first, second = reduce_hidden(
            mdot(u_full, weights_in), mdot(v_full, weights) + mdot(u_full, dirs), x, z, True
        )
        if step == 0:
            c_y = after(c_y, first)
            back = reduce_hidden_aside(
                jnp.concatenate([mdot(c_y, down), mdot(t_c_y, down) + mdot(c_y, dir_down)], axis=1)
            )
            c_h, t_c_h = halves(back)
        sum_sq = first[:, HID : HID + 1] + first[:, HID + 1 : HID + 2]
        sum_tan = first[:, HID + 2 : HID + 3] + first[:, HID + 3 : HID + 4]
        r_val = lax.rsqrt(sum_sq / D + EPS)
        t_r = -0.5 * r_val * r_val * r_val * (2.0 * sum_tan / D)
        u_g, u_u = halves(first)
        v_g, v_u = halves(second)
        pre = (r_val * u_g, r_val * u_u, r_val * v_g + t_r * u_g, r_val * v_u + t_r * u_u)
        h_val, t_h = hidden_forward(*pre)
        h_val = pad_to(h_val.astype(BF), 16, SPAN)
        t_h = pad_to(t_h.astype(BF), 16, SPAN)
        if step < ITERS - 1:
            h_full, t_h_full = gather_hidden(h_val, t_h, x, z)
            y_val, t_y = reduce_features(
                inner_cols(h_full, down), inner_cols(t_h_full, down) + inner_cols(h_full, dir_down)
            )
            state = state + y_val
            t_state = t_state + t_y
            hidden = (h_full, t_h_full)
        else:
            hidden = jnp.concatenate([h_val, t_h], axis=1)
        saved.append((a_val, t_a, stats, r_val, t_r, u_full, v_full, pre, hidden))
    acc = jnp.zeros((WIDE, 2 * SPAN), F32)
    acc_down = jnp.zeros((WIDE, SPAN), F32)
    for step in reversed(range(ITERS)):
        a_val, t_a, stats, r_val, t_r, u_full, v_full, pre, hidden = saved[step]
        if step < ITERS - 1:
            c_y, t_c_y = gather_tokens(token_block(c_state, t_c_state))
            c_h, t_c_h = reduce_hidden(mdot(c_y, down), mdot(t_c_y, down) + mdot(c_y, dir_down), x, z)
        c_pg, c_pu, t_c_pg, t_c_pu = hidden_backward(*pre, c_h[:, :HID], t_c_h[:, :HID])
        c_v, c_u = gather_hidden(
            joined(r_val * c_pg, r_val * c_pu),
            joined(t_r * c_pg + r_val * t_c_pg, t_r * c_pu + r_val * t_c_pu),
            x,
            z,
        )
        acc = acc + inner_rows(v_full, c_v) + inner_rows(u_full, c_u)
        q_val, t_q = reduce_features(
            inner_cols(c_v, weights), inner_cols(c_u, weights) + inner_cols(c_v, dirs)
        )
        if step == ITERS - 1:
            full = lax.all_gather(after(hidden, q_val), "col", axis=0, tiled=True)
            hidden = (full[:, :SPAN], full[:, SPAN:])
        acc_down = acc_down + inner_rows(c_y, hidden[1]) + inner_rows(t_c_y, hidden[0])
        q_val = gain * q_val
        t_q = gain * t_q
        sums = sum_col(
            jnp.concatenate(
                [stats[0], stats[1], row_sum(a_val * q_val), row_sum(t_a * q_val + a_val * t_q)], axis=1
            )
        )
        r_sq = 1.0 / (sums[:, 0:1] / D + EPS)
        r_t_r = -r_sq * r_sq * sums[:, 1:2] / D
        beta = r_sq * sums[:, 2:3] / D
        alpha = (2.0 * r_t_r * sums[:, 2:3] + r_sq * sums[:, 3:4]) / D
        c_state = c_state + q_val - beta * a_val
        t_c_state = t_c_state + t_q - alpha * a_val - beta * t_a
    gate_est = (2 * gate_sign - 1).astype(F32) * acc[:FEAT, :HID]
    up_est = (2 * up_sign - 1).astype(F32) * acc[:FEAT, SPAN : SPAN + HID]
    down_est = (2 * down_sign - 1).astype(F32) * acc_down[:FEAT, :HID].T
    return (gate_est, up_est, down_est)


def solution(mesh):
    return jax.shard_map(
        per_device,
        mesh=mesh,
        in_specs=(
            P("row", "col"),
            P("row", "col"),
            P("row", "col"),
            P("col"),
            P("col", "row"),
            P("col", "row"),
            P("row", "col"),
            P("col", "row"),
            P("col", "row"),
            P("row", "col"),
        ),
        out_specs=(P("col", "row"), P("col", "row"), P("row", "col")),
        check_vma=False,
    )
```

```python
import jax
import jax.numpy as jnp
from jax import lax
from jax.sharding import PartitionSpec as P

D = 5280
FF = 17920
ITERS = 2
EPS = 1e-06

FEAT = 330
WIDE = 384
HID = 1120
SPAN = 1152
BF = jnp.bfloat16
F32 = jnp.float32

AT_X = [[(z * 4 + x, z * 4 + (x + k) % 4) for z in range(4) for x in range(4)] for k in range(4)]
AT_Z = [[(z * 4 + x, (z + k) % 4 * 4 + x) for z in range(4) for x in range(4)] for k in range(4)]
OTHER_CORE = [(i, i ^ 1) for i in range(16)]
OTHER_Z = [(i, i ^ 8) for i in range(16)]
AT_Y = [[(i, i // 8 * 8 + (i + 2 * k) % 8) for i in range(16)] for k in range(4)]


def mdot(left, right):
    return jnp.dot(left, right, preferred_element_type=F32)


def inner_rows(left, right):
    return lax.dot_general(left, right, (((0,), (0,)), ((), ())), preferred_element_type=F32)


def inner_cols(left, right):
    return lax.dot_general(left, right, (((1,), (1,)), ((), ())), preferred_element_type=F32)


def direction(sign, fan_in):
    return ((2 * sign - 1).astype(F32) * float(fan_in) ** (-0.5)).astype(BF)


def pad_to(array, rows, columns):
    return jnp.pad(array, ((0, rows - array.shape[0]), (0, columns - array.shape[1])))


def side_by_side(first, second):
    return jnp.concatenate([pad_to(first, WIDE, SPAN), pad_to(second, WIDE, SPAN)], axis=1)


def with_spare(array, wide, values):
    at = array.shape[1]
    array = pad_to(array, array.shape[0], wide)
    lane = lax.broadcasted_iota(jnp.int32, array.shape, 1)
    for value in values:
        high = lax.reduce_precision(value, 8, 7)
        array = jnp.where(lane == at, high, jnp.where(lane == at + 1, value - high, array))
        at += 2
    return array.astype(BF)


def exchange_sum(chunks, axis, place, perms, mesh_axis="col"):
    pieces = lax.optimization_barrier(
        tuple(lax.dynamic_index_in_dim(chunks, (place + k) % 4, axis, keepdims=False) for k in range(4))
    )
    got = lax.optimization_barrier(tuple(lax.ppermute(pieces[k], mesh_axis, perms[k]) for k in range(1, 4)))
    total = pieces[0].astype(F32)
    for piece in got:
        total = total + piece.astype(F32)
    return total


def reduce_x(partial, x):
    return exchange_sum(partial.astype(BF).reshape(4, 4, 16, -1), 1, x, AT_X).astype(BF)


def reduce_z(partial, z):
    return exchange_sum(partial, 0, z, AT_Z)


def reduce_and_gather_z(partial, block, z):
    width = partial.shape[2]
    pieces = lax.optimization_barrier(
        tuple(
            jnp.concatenate([lax.dynamic_index_in_dim(partial, (z + k) % 4, 0, keepdims=False), block], axis=1)
            for k in range(4)
        )
    )
    got = lax.optimization_barrier(tuple(lax.ppermute(pieces[k], "col", AT_Z[k]) for k in range(1, 4)))
    total = pieces[0][:, :width].astype(F32)
    for piece in got:
        total = total + piece[:, :width].astype(F32)
    return total, place_all(block, tuple(piece[:, width:] for piece in got), z, 0)


def place_all(own, got, place, axis):
    shape = own.shape[:axis] + (4,) + own.shape[axis:]
    out = jnp.zeros(shape, own.dtype)
    for k, piece in enumerate((own,) + got):
        out = lax.dynamic_update_slice_in_dim(out, jnp.expand_dims(piece, axis), (place - k) % 4, axis)
    return out


def gather_z(block, z, widths):
    got = lax.optimization_barrier(tuple(lax.ppermute(block, "col", AT_Z[k]) for k in range(1, 4)))
    outs, low = [], 0
    for width in widths:
        outs.append(place_all(block[:, low : low + width], tuple(g[:, low : low + width] for g in got), z, 0))
        low += width
    return outs


def gather_x(block, x):
    got = lax.optimization_barrier(tuple(lax.ppermute(block, "col", AT_X[k]) for k in range(1, 4)))
    return place_all(block, got, x, 1).reshape(256, -1)


def after(array, other):
    return array + (0.0 * other.reshape(-1, other.shape[-1])[:1, :1].astype(F32)).astype(array.dtype)


def halve(array, axis, bit, perm):
    keep = lax.dynamic_index_in_dim(array, bit, axis, keepdims=False)
    send = lax.dynamic_index_in_dim(array, 1 - bit, axis, keepdims=False)
    return (keep.astype(F32) + lax.ppermute(send, "row", perm).astype(F32)).astype(BF)


def row_place():
    place = lax.axis_index("row")
    return place // 8, place // 2 % 4, place % 2


def reduce_features(first, second):
    z, y, core = row_place()
    partial = jnp.concatenate([first, second], axis=1).astype(BF).reshape(2, 4, 2, 16, 2 * WIDE)
    partial = halve(partial, 2, core, OTHER_CORE)
    partial = halve(partial, 0, z, OTHER_Z)
    total = exchange_sum(partial, 0, y, AT_Y, "row")
    return total[:, :FEAT], total[:, WIDE : WIDE + FEAT], total[:, FEAT : FEAT + 8]


def token_block(first, second, stats=()):
    return jnp.concatenate([with_spare(first, WIDE, stats), with_spare(second, WIDE, ())], axis=1)


def twice(block, bit, perm):
    got = lax.ppermute(block, "row", perm)
    return jnp.where(bit == 0, jnp.stack([block, got]), jnp.stack([got, block]))


def gather_tokens(block):
    z, y, core = row_place()
    block = twice(twice(block, core, OTHER_CORE), z, OTHER_Z)
    got = lax.optimization_barrier(tuple(lax.ppermute(block, "row", AT_Y[k]) for k in range(1, 4)))
    full = place_all(block, got, y, 1).reshape(256, -1)
    return tuple(full[:, at : at + WIDE] for at in range(0, full.shape[1], WIDE))


def halves(array):
    return array[:, :HID], array[:, SPAN : SPAN + HID]


def joined(first, second, spare=()):
    return jnp.concatenate([with_spare(first, SPAN, ()), with_spare(second, SPAN, spare)], axis=1)


def hidden_forward(pg, pu, t_pg, t_pu):
    sg = jax.nn.sigmoid(pg)
    act = pg * sg
    slope = sg * (1.0 + pg * (1.0 - sg))
    return act * pu, slope * t_pg * pu + act * t_pu


def hidden_backward(pg, pu, t_pg, t_pu, c_h, t_c_h):
    sg = jax.nn.sigmoid(pg)
    act = pg * sg
    slope = sg * (1.0 + pg * (1.0 - sg))
    curve = sg * (1.0 - sg) * (2.0 + pg * (1.0 - 2.0 * sg))
    c_pg = c_h * pu * slope
    c_pu = c_h * act
    t_c_pg = t_c_h * pu * slope + c_h * t_pu * slope + c_h * pu * curve * t_pg
    t_c_pu = t_c_h * act + c_h * slope * t_pg
    return c_pg, c_pu, t_c_pg, t_c_pu


def row_sum(array):
    return jnp.sum(array, axis=-1, keepdims=True)


def per_device(
    latent,
    embedded,
    cotangent,
    gain,
    gate_weight,
    up_weight,
    down_weight,
    gate_sign,
    up_sign,
    down_sign,
):
    place = lax.axis_index("col")
    x = place % 4
    z = place // 4
    weights = side_by_side(gate_weight, up_weight)
    row = lax.broadcasted_iota(jnp.int32, (WIDE, 2 * SPAN), 0) - FEAT
    column = lax.broadcasted_iota(jnp.int32, (WIDE, 2 * SPAN), 1)
    onward = (row >= 0) & (row < 4) & (column - HID - 4 * x == row)
    back = (row >= 0) & (row < 8) & (column - SPAN - HID == row)
    weights = jnp.where(onward | back, jnp.ones((), BF), weights)
    dirs = side_by_side(direction(gate_sign, D), direction(up_sign, D))
    down = pad_to(down_weight.T, WIDE, SPAN)
    dir_down = pad_to(direction(down_sign.T, FF), WIDE, SPAN)

    state = latent
    t_state = jnp.zeros_like(latent)
    c_state = cotangent
    t_c_state = jnp.zeros_like(cotangent)
    saved = []
    for step in range(ITERS):
        a_val = state + embedded
        t_a = t_state
        stats = (row_sum(a_val * a_val), row_sum(a_val * t_a))
        block = token_block(a_val * gain, t_a * gain, stats)
        if step == 0:
            u_full, v_full, c_y, t_c_y = gather_tokens(
                jnp.concatenate([block, token_block(c_state, t_c_state)], axis=1)
            )
        else:
            u_full, v_full = gather_tokens(block)
            u_full = after(u_full, back)
        first = reduce_x(mdot(u_full, weights), x)
        second = reduce_x(mdot(v_full, weights) + mdot(u_full, dirs), x)
        first = reduce_z(first, z)
        if step > 0:
            second = jnp.concatenate([second, back], axis=2)
        second = reduce_z(second, z)
        if step == 0:
            aside = jnp.concatenate([mdot(c_y, down), mdot(t_c_y, down) + mdot(c_y, dir_down)], axis=1).astype(BF)
        else:
            c_h, t_c_h = second[:, 2 * SPAN : 3 * SPAN], second[:, 3 * SPAN :]
        spare = first[:, HID:SPAN]
        column = lax.broadcasted_iota(jnp.int32, spare.shape, 1)
        sum_sq = row_sum(jnp.where((column < 16) & (column % 4 < 2), spare, 0.0))
        sum_tan = row_sum(jnp.where((column < 16) & (column % 4 >= 2), spare, 0.0))
        r_val = lax.rsqrt(sum_sq / D + EPS)
        t_r = -0.5 * r_val * r_val * r_val * (2.0 * sum_tan / D)
        u_g, u_u = halves(first)
        v_g, v_u = halves(second)
        pre = (r_val * u_g, r_val * u_u, r_val * v_g + t_r * u_g, r_val * v_u + t_r * u_u)
        h_val, t_h = hidden_forward(*pre)
        hidden = joined(h_val, t_h)
        if step < ITERS - 1:
            (part,) = gather_z(hidden, z, (2 * SPAN,))
            full = gather_x(part, x)
            h_full, t_h_full = full[:, :SPAN], full[:, SPAN:]
            back = reduce_x(after(aside, full), x)
            y_val, t_y, _ = reduce_features(
                inner_cols(h_full, down), inner_cols(t_h_full, down) + inner_cols(h_full, dir_down)
            )
            state = state + y_val
            t_state = t_state + t_y
            hidden = (h_full, t_h_full)
        saved.append((a_val, t_a, r_val, t_r, (u_g, u_u, v_g, v_u), u_full, v_full, pre, hidden))
    acc = jnp.zeros((WIDE, 2 * SPAN), F32)
    acc_down = jnp.zeros((WIDE, SPAN), F32)
    for step in reversed(range(ITERS)):
        a_val, t_a, r_val, t_r, raw, u_full, v_full, pre, hidden = saved[step]
        if step < ITERS - 1:
            c_y, t_c_y = gather_tokens(token_block(c_state, t_c_state))
            part = jnp.concatenate([mdot(c_y, down), mdot(t_c_y, down) + mdot(c_y, dir_down)], axis=1)
            part, last_h = reduce_and_gather_z(reduce_x(part, x), last_hidden, z)
            c_h, t_c_h = halves(part)
            last_h = gather_x(last_h, x)
            acc_down = acc_down + inner_rows(last_c_y[0], last_h[:, SPAN:]) + inner_rows(last_c_y[1], last_h[:, :SPAN])
        c_pg, c_pu, t_c_pg, t_c_pu = hidden_backward(*pre, c_h[:, :HID], t_c_h[:, :HID])
        v_c = (r_val * c_pg, r_val * c_pu)
        u_c = (t_r * c_pg + r_val * t_c_pg, t_r * c_pu + r_val * t_c_pu)
        spare = ()
        if step > 0:
            u_g, u_u, v_g, v_u = raw
            spare = (
                row_sum(v_c[0] * u_g + v_c[1] * u_u),
                row_sum(v_c[0] * v_g + v_c[1] * v_u + u_c[0] * u_g + u_c[1] * u_u),
                r_val * r_val,
                r_val * t_r,
            )
        (c_v,) = gather_z(joined(*v_c, spare), z, (2 * SPAN,))
        (c_u,) = gather_z(joined(*u_c), z, (2 * SPAN,))
        if step == 0:
            c_v = after(c_v, last_h)
        c_v = gather_x(c_v, x)
        c_u = gather_x(c_u, x)
        if step == 0:
            acc_down = acc_down + inner_rows(c_y, hidden[1]) + inner_rows(t_c_y, hidden[0])
            u_full = after(u_full, acc_down)
        acc = acc + inner_rows(v_full, c_v) + inner_rows(u_full, c_u)
        if step > 0:
            q_val, t_q, sums = reduce_features(
                inner_cols(c_v, weights), inner_cols(c_u, weights) + inner_cols(c_v, dirs)
            )
            last_hidden = hidden
            last_c_y = (c_y, t_c_y)
            q_val = gain * q_val
            t_q = gain * t_q
            s_val, s_tan, r_sq, r_t_r = (sums[:, k : k + 1] + sums[:, k + 1 : k + 2] for k in (0, 2, 4, 6))
            r_sq = r_sq / 16
            r_t_r = r_t_r / 16
            beta = r_sq * s_val / D
            alpha = (2.0 * r_t_r * s_val + r_sq * s_tan) / D
            c_state = c_state + q_val - beta * a_val
            t_c_state = t_c_state + t_q - alpha * a_val - beta * t_a
    gate_est = (2 * gate_sign - 1).astype(F32) * acc[:FEAT, :HID]
    up_est = (2 * up_sign - 1).astype(F32) * acc[:FEAT, SPAN : SPAN + HID]
    down_est = (2 * down_sign - 1).astype(F32) * acc_down[:FEAT, :HID].T
    return (gate_est, up_est, down_est)


def solution(mesh):
    return jax.shard_map(
        per_device,
        mesh=mesh,
        in_specs=(
            P("row", "col"),
            P("row", "col"),
            P("row", "col"),
            P("col"),
            P("col", "row"),
            P("col", "row"),
            P("row", "col"),
            P("col", "row"),
            P("col", "row"),
            P("row", "col"),
        ),
        out_specs=(P("col", "row"), P("col", "row"), P("row", "col")),
        check_vma=False,
    )
```

```python
import jax
import jax.numpy as jnp
from jax import lax
from jax.sharding import PartitionSpec as P

D = 5280
FF = 17920
ITERS = 2
EPS = 1e-06

FEAT = 330
WIDE = 384
HID = 1120
SPAN = 1152
BF = jnp.bfloat16
F32 = jnp.float32

AT_X = [[(z * 4 + x, z * 4 + (x + k) % 4) for z in range(4) for x in range(4)] for k in range(4)]
AT_Z = [[(z * 4 + x, (z + k) % 4 * 4 + x) for z in range(4) for x in range(4)] for k in range(4)]
OTHER_CORE = [(i, i ^ 1) for i in range(16)]
OTHER_Z = [(i, i ^ 8) for i in range(16)]
AT_Y = [[(i, i // 8 * 8 + (i + 2 * k) % 8) for i in range(16)] for k in range(4)]


def mdot(left, right):
    return jnp.dot(left, right, preferred_element_type=F32)


def inner_rows(left, right):
    return lax.dot_general(left, right, (((0,), (0,)), ((), ())), preferred_element_type=F32)


def inner_cols(left, right):
    return lax.dot_general(left, right, (((1,), (1,)), ((), ())), preferred_element_type=F32)


def direction(sign, fan_in):
    return ((2 * sign - 1).astype(F32) * float(fan_in) ** (-0.5)).astype(BF)


def pad_to(array, rows, columns):
    return jnp.pad(array, ((0, rows - array.shape[0]), (0, columns - array.shape[1])))


def side_by_side(first, second):
    return jnp.concatenate([pad_to(first, WIDE, SPAN), pad_to(second, WIDE, SPAN)], axis=1)


def with_spare(array, wide, values):
    at = array.shape[1]
    array = pad_to(array, array.shape[0], wide)
    lane = lax.broadcasted_iota(jnp.int32, array.shape, 1)
    for value in values:
        high = lax.reduce_precision(value, 8, 7)
        array = jnp.where(lane == at, high, jnp.where(lane == at + 1, value - high, array))
        at += 2
    return array.astype(BF)


def exchange_sum(chunks, axis, place, perms):
    pieces = lax.optimization_barrier(
        tuple(lax.dynamic_index_in_dim(chunks, (place + k) % 4, axis, keepdims=False) for k in range(4))
    )
    got = lax.optimization_barrier(tuple(lax.ppermute(pieces[k], "col", perms[k]) for k in range(1, 4)))
    total = pieces[0].astype(F32)
    for piece in got:
        total = total + piece.astype(F32)
    return total


def reduce_x(partial, x):
    return exchange_sum(partial.astype(BF).reshape(4, 4, 16, -1), 1, x, AT_X).astype(BF)


def reduce_z(partial, z):
    return exchange_sum(partial, 0, z, AT_Z)


def reduce_and_gather_z(partial, block, z):
    width = partial.shape[2]
    pieces = lax.optimization_barrier(
        tuple(
            jnp.concatenate([lax.dynamic_index_in_dim(partial, (z + k) % 4, 0, keepdims=False), block], axis=1)
            for k in range(4)
        )
    )
    got = lax.optimization_barrier(tuple(lax.ppermute(pieces[k], "col", AT_Z[k]) for k in range(1, 4)))
    total = pieces[0][:, :width].astype(F32)
    for piece in got:
        total = total + piece[:, :width].astype(F32)
    return total, place_all(block, tuple(piece[:, width:] for piece in got), z, 0)


def place_all(own, got, place, axis):
    shape = own.shape[:axis] + (4,) + own.shape[axis:]
    out = jnp.zeros(shape, own.dtype)
    for k, piece in enumerate((own,) + got):
        out = lax.dynamic_update_slice_in_dim(out, jnp.expand_dims(piece, axis), (place - k) % 4, axis)
    return out


def gather_z(block, z, widths):
    got = lax.optimization_barrier(tuple(lax.ppermute(block, "col", AT_Z[k]) for k in range(1, 4)))
    outs, low = [], 0
    for width in widths:
        outs.append(place_all(block[:, low : low + width], tuple(g[:, low : low + width] for g in got), z, 0))
        low += width
    return outs


def gather_x(block, x):
    got = lax.optimization_barrier(tuple(lax.ppermute(block, "col", AT_X[k]) for k in range(1, 4)))
    return place_all(block, got, x, 1).reshape(256, -1)


def after(array, other):
    return array + (0.0 * other.reshape(-1, other.shape[-1])[:1, :1].astype(F32)).astype(array.dtype)


def halve(array, axis, bit, perm):
    keep = lax.dynamic_index_in_dim(array, bit, axis, keepdims=False)
    send = lax.dynamic_index_in_dim(array, 1 - bit, axis, keepdims=False)
    return (keep.astype(F32) + lax.ppermute(send, "row", perm).astype(F32)).astype(BF)


def row_place():
    place = lax.axis_index("row")
    return place // 8, place // 2 % 4, place % 2


def reduce_features(first, second):
    z, _, core = row_place()
    partial = jnp.concatenate([first, second], axis=1).astype(BF).reshape(2, 4, 2, 16, 2 * WIDE)
    partial = halve(partial, 2, core, OTHER_CORE)
    partial = halve(partial, 0, z, OTHER_Z)
    got = lax.optimization_barrier(tuple(lax.ppermute(partial, "row", AT_Y[k]) for k in range(1, 4)))
    total = partial.astype(F32)
    for piece in got:
        total = total + piece.astype(F32)
    total = total.reshape(64, 2 * WIDE)
    return total[:, :FEAT], total[:, WIDE : WIDE + FEAT], total[:, FEAT : FEAT + 8]


def token_block(first, second, stats=()):
    return jnp.concatenate([with_spare(first, WIDE, stats), with_spare(second, WIDE, ())], axis=1)


def gather_y(block):
    got = lax.optimization_barrier(tuple(lax.ppermute(block, "row", AT_Y[k]) for k in range(1, 4)))
    return place_all(block, got, row_place()[1], 0).reshape(64, -1)


def twice(block, axis, bit, perm):
    got = lax.ppermute(block, "row", perm)
    return jnp.where(bit == 0, jnp.stack([block, got], axis), jnp.stack([got, block], axis))


def gather_tokens(block):
    z, _, core = row_place()
    block = twice(block.reshape(4, 16, -1), 0, z, OTHER_Z)
    full = twice(block, 2, core, OTHER_CORE).reshape(256, -1)
    return tuple(full[:, at : at + WIDE] for at in range(0, full.shape[1], WIDE))


def halves(array):
    return array[:, :HID], array[:, SPAN : SPAN + HID]


def joined(first, second, spare=()):
    return jnp.concatenate([with_spare(first, SPAN, ()), with_spare(second, SPAN, spare)], axis=1)


def hidden_forward(pg, pu, t_pg, t_pu):
    sg = jax.nn.sigmoid(pg)
    act = pg * sg
    slope = sg * (1.0 + pg * (1.0 - sg))
    return act * pu, slope * t_pg * pu + act * t_pu


def hidden_backward(pg, pu, t_pg, t_pu, c_h, t_c_h):
    sg = jax.nn.sigmoid(pg)
    act = pg * sg
    slope = sg * (1.0 + pg * (1.0 - sg))
    curve = sg * (1.0 - sg) * (2.0 + pg * (1.0 - 2.0 * sg))
    c_pg = c_h * pu * slope
    c_pu = c_h * act
    t_c_pg = t_c_h * pu * slope + c_h * t_pu * slope + c_h * pu * curve * t_pg
    t_c_pu = t_c_h * act + c_h * slope * t_pg
    return c_pg, c_pu, t_c_pg, t_c_pu


def row_sum(array):
    return jnp.sum(array, axis=-1, keepdims=True)


def per_device(
    latent,
    embedded,
    cotangent,
    gain,
    gate_weight,
    up_weight,
    down_weight,
    gate_sign,
    up_sign,
    down_sign,
):
    place = lax.axis_index("col")
    x = place % 4
    z = place // 4
    weights = side_by_side(gate_weight, up_weight)
    row = lax.broadcasted_iota(jnp.int32, (WIDE, 2 * SPAN), 0) - FEAT
    column = lax.broadcasted_iota(jnp.int32, (WIDE, 2 * SPAN), 1)
    onward = (row >= 0) & (row < 4) & (column - HID - 4 * x == row)
    back = (row >= 0) & (row < 8) & (column - SPAN - HID == row)
    weights = jnp.where(onward | back, jnp.ones((), BF), weights)
    dirs = side_by_side(direction(gate_sign, D), direction(up_sign, D))
    down = pad_to(down_weight.T, WIDE, SPAN)
    dir_down = pad_to(direction(down_sign.T, FF), WIDE, SPAN)

    own = jnp.concatenate([pad_to(latent + embedded, 16, WIDE), pad_to(cotangent, 16, WIDE)], axis=1)
    own = gather_y(own)
    a_val = own[:, :FEAT]
    c_state = own[:, WIDE : WIDE + FEAT]
    t_a = jnp.zeros_like(a_val)
    t_c_state = jnp.zeros_like(c_state)
    saved = []
    for step in range(ITERS):
        stats = (row_sum(a_val * a_val), row_sum(a_val * t_a))
        block = token_block(a_val * gain, t_a * gain, stats)
        if step == 0:
            u_full, v_full, c_y, t_c_y = gather_tokens(
                jnp.concatenate([block, token_block(c_state, t_c_state)], axis=1)
            )
        else:
            u_full, v_full = gather_tokens(block)
            u_full = after(u_full, back)
        first = reduce_x(mdot(u_full, weights), x)
        second = reduce_x(mdot(v_full, weights) + mdot(u_full, dirs), x)
        first = reduce_z(first, z)
        if step > 0:
            second = jnp.concatenate([second, back], axis=2)
        second = reduce_z(second, z)
        if step == 0:
            aside = jnp.concatenate([mdot(c_y, down), mdot(t_c_y, down) + mdot(c_y, dir_down)], axis=1).astype(BF)
        else:
            c_h, t_c_h = second[:, 2 * SPAN : 3 * SPAN], second[:, 3 * SPAN :]
        spare = first[:, HID:SPAN]
        column = lax.broadcasted_iota(jnp.int32, spare.shape, 1)
        sum_sq = row_sum(jnp.where((column < 16) & (column % 4 < 2), spare, 0.0))
        sum_tan = row_sum(jnp.where((column < 16) & (column % 4 >= 2), spare, 0.0))
        r_val = lax.rsqrt(sum_sq / D + EPS)
        t_r = -0.5 * r_val * r_val * r_val * (2.0 * sum_tan / D)
        u_g, u_u = halves(first)
        v_g, v_u = halves(second)
        pre = (r_val * u_g, r_val * u_u, r_val * v_g + t_r * u_g, r_val * v_u + t_r * u_u)
        h_val, t_h = hidden_forward(*pre)
        hidden = joined(h_val, t_h)
        if step < ITERS - 1:
            (part,) = gather_z(hidden, z, (2 * SPAN,))
            full = gather_x(part, x)
            h_full, t_h_full = full[:, :SPAN], full[:, SPAN:]
            back = reduce_x(after(aside, full), x)
            y_val, t_y, _ = reduce_features(
                inner_cols(h_full, down), inner_cols(t_h_full, down) + inner_cols(h_full, dir_down)
            )
            hidden = (h_full, t_h_full)
        saved.append((a_val, t_a, r_val, t_r, (u_g, u_u, v_g, v_u), u_full, v_full, pre, hidden))
        if step < ITERS - 1:
            a_val = a_val + y_val
            t_a = t_a + t_y
    acc = jnp.zeros((WIDE, 2 * SPAN), F32)
    acc_down = jnp.zeros((WIDE, SPAN), F32)
    for step in reversed(range(ITERS)):
        a_val, t_a, r_val, t_r, raw, u_full, v_full, pre, hidden = saved[step]
        if step < ITERS - 1:
            c_y, t_c_y = gather_tokens(token_block(c_state, t_c_state))
            part = jnp.concatenate([mdot(c_y, down), mdot(t_c_y, down) + mdot(c_y, dir_down)], axis=1)
            part, last_h = reduce_and_gather_z(reduce_x(part, x), last_hidden, z)
            c_h, t_c_h = halves(part)
            last_h = gather_x(last_h, x)
            acc_down = acc_down + inner_rows(last_c_y[0], last_h[:, SPAN:]) + inner_rows(last_c_y[1], last_h[:, :SPAN])
        c_pg, c_pu, t_c_pg, t_c_pu = hidden_backward(*pre, c_h[:, :HID], t_c_h[:, :HID])
        v_c = (r_val * c_pg, r_val * c_pu)
        u_c = (t_r * c_pg + r_val * t_c_pg, t_r * c_pu + r_val * t_c_pu)
        spare = ()
        if step > 0:
            u_g, u_u, v_g, v_u = raw
            spare = (
                row_sum(v_c[0] * u_g + v_c[1] * u_u),
                row_sum(v_c[0] * v_g + v_c[1] * v_u + u_c[0] * u_g + u_c[1] * u_u),
                r_val * r_val,
                r_val * t_r,
            )
        (c_v,) = gather_z(joined(*v_c, spare), z, (2 * SPAN,))
        (c_u,) = gather_z(joined(*u_c), z, (2 * SPAN,))
        if step == 0:
            c_v = after(c_v, last_h)
        c_v = gather_x(c_v, x)
        c_u = gather_x(c_u, x)
        if step == 0:
            acc_down = acc_down + inner_rows(c_y, hidden[1]) + inner_rows(t_c_y, hidden[0])
            u_full = after(u_full, acc_down)
        acc = acc + inner_rows(v_full, c_v) + inner_rows(u_full, c_u)
        if step > 0:
            q_val, t_q, sums = reduce_features(
                inner_cols(c_v, weights), inner_cols(c_u, weights) + inner_cols(c_v, dirs)
            )
            last_hidden = hidden
            last_c_y = (c_y, t_c_y)
            q_val = gain * q_val
            t_q = gain * t_q
            s_val, s_tan, r_sq, r_t_r = (sums[:, k : k + 1] + sums[:, k + 1 : k + 2] for k in (0, 2, 4, 6))
            r_sq = r_sq / 16
            r_t_r = r_t_r / 16
            beta = r_sq * s_val / D
            alpha = (2.0 * r_t_r * s_val + r_sq * s_tan) / D
            c_state = c_state + q_val - beta * a_val
            t_c_state = t_c_state + t_q - alpha * a_val - beta * t_a
    gate_est = (2 * gate_sign - 1).astype(F32) * acc[:FEAT, :HID]
    up_est = (2 * up_sign - 1).astype(F32) * acc[:FEAT, SPAN : SPAN + HID]
    down_est = (2 * down_sign - 1).astype(F32) * acc_down[:FEAT, :HID].T
    return (gate_est, up_est, down_est)


def solution(mesh):
    return jax.shard_map(
        per_device,
        mesh=mesh,
        in_specs=(
            P("row", "col"),
            P("row", "col"),
            P("row", "col"),
            P("col"),
            P("col", "row"),
            P("col", "row"),
            P("row", "col"),
            P("col", "row"),
            P("col", "row"),
            P("row", "col"),
        ),
        out_specs=(P("col", "row"), P("col", "row"), P("row", "col")),
        check_vma=False,
    )
```

```python
import jax
import jax.numpy as jnp
from jax import lax
from jax.sharding import PartitionSpec as P

D = 5280
FF = 17920
ITERS = 2
EPS = 1e-06

FEAT = 330
WIDE = 384
HID = 1120
SPAN = 1152
BF = jnp.bfloat16
F32 = jnp.float32

AT_X = [[(z * 4 + x, z * 4 + (x + k) % 4) for z in range(4) for x in range(4)] for k in range(4)]
AT_Z = [[(z * 4 + x, (z + k) % 4 * 4 + x) for z in range(4) for x in range(4)] for k in range(4)]
OTHER_CORE = [(i, i ^ 1) for i in range(16)]
OTHER_Z = [(i, i ^ 8) for i in range(16)]
AT_Y = [[(i, i // 8 * 8 + (i + 2 * k) % 8) for i in range(16)] for k in range(4)]


def mdot(left, right):
    return jnp.dot(left, right, preferred_element_type=F32)


def inner_rows(left, right):
    return lax.dot_general(left, right, (((0,), (0,)), ((), ())), preferred_element_type=F32)


def inner_cols(left, right):
    return lax.dot_general(left, right, (((1,), (1,)), ((), ())), preferred_element_type=F32)


def direction(sign, fan_in):
    return ((2 * sign - 1).astype(F32) * float(fan_in) ** (-0.5)).astype(BF)


def pad_to(array, rows, columns):
    return jnp.pad(array, ((0, rows - array.shape[0]), (0, columns - array.shape[1])))


def side_by_side(first, second):
    return jnp.concatenate([pad_to(first, WIDE, SPAN), pad_to(second, WIDE, SPAN)], axis=1)


def with_spare(array, wide, values):
    at = array.shape[1]
    array = pad_to(array, array.shape[0], wide)
    lane = lax.broadcasted_iota(jnp.int32, array.shape, 1)
    for value in values:
        high = lax.reduce_precision(value, 8, 7)
        array = jnp.where(lane == at, high, jnp.where(lane == at + 1, value - high, array))
        at += 2
    return array.astype(BF)


def exchange_sum(chunks, axis, place, perms):
    pieces = lax.optimization_barrier(
        tuple(lax.dynamic_index_in_dim(chunks, (place + k) % 4, axis, keepdims=False) for k in range(4))
    )
    got = lax.optimization_barrier(tuple(lax.ppermute(pieces[k], "col", perms[k]) for k in range(1, 4)))
    total = pieces[0].astype(F32)
    for piece in got:
        total = total + piece.astype(F32)
    return total


def reduce_x(partial, x):
    return exchange_sum(partial.astype(BF).reshape(4, 4, 16, -1), 1, x, AT_X).astype(BF)


def reduce_z(partial, z):
    return exchange_sum(partial, 0, z, AT_Z)


def reduce_and_gather_z(partial, block, z):
    width = partial.shape[2]
    pieces = lax.optimization_barrier(
        tuple(
            jnp.concatenate([lax.dynamic_index_in_dim(partial, (z + k) % 4, 0, keepdims=False), block], axis=1)
            for k in range(4)
        )
    )
    got = lax.optimization_barrier(tuple(lax.ppermute(pieces[k], "col", AT_Z[k]) for k in range(1, 4)))
    total = pieces[0][:, :width].astype(F32)
    for piece in got:
        total = total + piece[:, :width].astype(F32)
    return total, place_all(block, tuple(piece[:, width:] for piece in got), z, 0)


def place_all(own, got, place, axis):
    shape = own.shape[:axis] + (4,) + own.shape[axis:]
    out = jnp.zeros(shape, own.dtype)
    for k, piece in enumerate((own,) + got):
        out = lax.dynamic_update_slice_in_dim(out, jnp.expand_dims(piece, axis), (place - k) % 4, axis)
    return out


def gather_z(block, z, widths):
    got = lax.optimization_barrier(tuple(lax.ppermute(block, "col", AT_Z[k]) for k in range(1, 4)))
    outs, low = [], 0
    for width in widths:
        outs.append(place_all(block[:, low : low + width], tuple(g[:, low : low + width] for g in got), z, 0))
        low += width
    return outs


def gather_x(block, x):
    got = lax.optimization_barrier(tuple(lax.ppermute(block, "col", AT_X[k]) for k in range(1, 4)))
    return place_all(block, got, x, 1).reshape(256, -1)


def after(array, other):
    return array + (0.0 * other.reshape(-1, other.shape[-1])[:1, :1].astype(F32)).astype(array.dtype)


def halve(array, axis, bit, perm):
    keep = lax.dynamic_index_in_dim(array, bit, axis, keepdims=False)
    send = lax.dynamic_index_in_dim(array, 1 - bit, axis, keepdims=False)
    return (keep.astype(F32) + lax.ppermute(send, "row", perm).astype(F32)).astype(BF)


def row_place():
    place = lax.axis_index("row")
    return place // 8, place // 2 % 4, place % 2


def reduce_features(first, second):
    z, _, core = row_place()
    partial = jnp.concatenate([first, second], axis=1).astype(BF).reshape(2, 4, 2, 16, 2 * WIDE)
    partial = halve(partial, 2, core, OTHER_CORE)
    partial = halve(partial, 0, z, OTHER_Z)
    got = lax.optimization_barrier(tuple(lax.ppermute(partial, "row", AT_Y[k]) for k in range(1, 4)))
    total = partial.astype(F32)
    for piece in got:
        total = total + piece.astype(F32)
    total = total.reshape(64, 2 * WIDE)
    return total[:, :FEAT], total[:, WIDE : WIDE + FEAT], total[:, FEAT : FEAT + 8]


def token_block(first, second, stats=()):
    return jnp.concatenate([with_spare(first, WIDE, stats), with_spare(second, WIDE, ())], axis=1)


def gather_y(block):
    got = lax.optimization_barrier(tuple(lax.ppermute(block, "row", AT_Y[k]) for k in range(1, 4)))
    return place_all(block, got, row_place()[1], 0).reshape(64, -1)


def twice(block, axis, bit, perm):
    got = lax.ppermute(block, "row", perm)
    return jnp.where(bit == 0, jnp.stack([block, got], axis), jnp.stack([got, block], axis))


def gather_tokens(block):
    z, _, core = row_place()
    block = twice(block.reshape(4, 16, -1), 0, z, OTHER_Z)
    full = twice(block, 2, core, OTHER_CORE).reshape(256, -1)
    return tuple(full[:, at : at + WIDE] for at in range(0, full.shape[1], WIDE))


def halves(array):
    return array[:, :HID], array[:, SPAN : SPAN + HID]


def joined(first, second, spare=()):
    return jnp.concatenate([with_spare(first, SPAN, ()), with_spare(second, SPAN, spare)], axis=1)


def hidden_forward(pg, pu, t_pg, t_pu):
    sg = jax.nn.sigmoid(pg)
    act = pg * sg
    slope = sg * (1.0 + pg * (1.0 - sg))
    return act * pu, slope * t_pg * pu + act * t_pu


def hidden_backward(pg, pu, t_pg, t_pu, c_h, t_c_h):
    sg = jax.nn.sigmoid(pg)
    act = pg * sg
    slope = sg * (1.0 + pg * (1.0 - sg))
    curve = sg * (1.0 - sg) * (2.0 + pg * (1.0 - 2.0 * sg))
    c_pg = c_h * pu * slope
    c_pu = c_h * act
    t_c_pg = t_c_h * pu * slope + c_h * t_pu * slope + c_h * pu * curve * t_pg
    t_c_pu = t_c_h * act + c_h * slope * t_pg
    return c_pg, c_pu, t_c_pg, t_c_pu


def row_sum(array):
    return jnp.sum(array, axis=-1, keepdims=True)


def per_device(
    latent,
    embedded,
    cotangent,
    gain,
    gate_weight,
    up_weight,
    down_weight,
    gate_sign,
    up_sign,
    down_sign,
):
    place = lax.axis_index("col")
    x = place % 4
    z = place // 4
    weights = side_by_side(gate_weight, up_weight)
    row = lax.broadcasted_iota(jnp.int32, (WIDE, 2 * SPAN), 0) - FEAT
    column = lax.broadcasted_iota(jnp.int32, (WIDE, 2 * SPAN), 1)
    onward = (row >= 0) & (row < 4) & (column - HID - 4 * x == row)
    back = (row >= 0) & (row < 8) & (column - SPAN - HID == row)
    weights = jnp.where(onward | back, jnp.ones((), BF), weights)
    dirs = side_by_side(direction(gate_sign, D), direction(up_sign, D))
    down = pad_to(down_weight.T, WIDE, SPAN)
    dir_down = pad_to(direction(down_sign.T, FF), WIDE, SPAN)

    own = jnp.concatenate([pad_to(latent + embedded, 16, WIDE), pad_to(cotangent, 16, WIDE)], axis=1)
    own = gather_y(own)
    a_val = own[:, :FEAT]
    c_state = own[:, WIDE : WIDE + FEAT]
    t_a = jnp.zeros_like(a_val)
    t_c_state = jnp.zeros_like(c_state)
    saved = []
    for step in range(ITERS):
        stats = (row_sum(a_val * a_val), row_sum(a_val * t_a))
        block = token_block(a_val * gain, t_a * gain, stats)
        if step == 0:
            u_full, v_full, c_y, t_c_y = gather_tokens(
                jnp.concatenate([block, token_block(c_state, t_c_state)], axis=1)
            )
        else:
            u_full, v_full = gather_tokens(block)
            u_full = after(u_full, back)
        first = reduce_x(mdot(u_full, weights), x)
        second = reduce_x(mdot(v_full, weights) + mdot(u_full, dirs), x)
        if step > 0:
            first = jnp.concatenate([first, back[:, :, :SPAN]], axis=2)
            second = jnp.concatenate([second, back[:, :, SPAN:]], axis=2)
        first = reduce_z(first, z)
        second = reduce_z(second, z)
        if step == 0:
            aside = jnp.concatenate([mdot(c_y, down), mdot(t_c_y, down) + mdot(c_y, dir_down)], axis=1).astype(BF)
        else:
            c_h, t_c_h = first[:, 2 * SPAN :], second[:, 2 * SPAN :]
        spare = first[:, HID:SPAN]
        column = lax.broadcasted_iota(jnp.int32, spare.shape, 1)
        sum_sq = row_sum(jnp.where((column < 16) & (column % 4 < 2), spare, 0.0))
        sum_tan = row_sum(jnp.where((column < 16) & (column % 4 >= 2), spare, 0.0))
        r_val = lax.rsqrt(sum_sq / D + EPS)
        t_r = -0.5 * r_val * r_val * r_val * (2.0 * sum_tan / D)
        u_g, u_u = halves(first)
        v_g, v_u = halves(second)
        pre = (r_val * u_g, r_val * u_u, r_val * v_g + t_r * u_g, r_val * v_u + t_r * u_u)
        h_val, t_h = hidden_forward(*pre)
        hidden = joined(h_val, t_h)
        if step < ITERS - 1:
            (part,) = gather_z(hidden, z, (2 * SPAN,))
            full = gather_x(part, x)
            h_full, t_h_full = full[:, :SPAN], full[:, SPAN:]
            back = reduce_x(after(aside, full), x)
            y_val, t_y, _ = reduce_features(
                inner_cols(h_full, down), inner_cols(t_h_full, down) + inner_cols(h_full, dir_down)
            )
            hidden = (h_full, t_h_full)
        saved.append((a_val, t_a, r_val, t_r, (u_g, u_u, v_g, v_u), u_full, v_full, pre, hidden))
        if step < ITERS - 1:
            a_val = a_val + y_val
            t_a = t_a + t_y
    acc = jnp.zeros((WIDE, 2 * SPAN), F32)
    acc_down = jnp.zeros((WIDE, SPAN), F32)
    for step in reversed(range(ITERS)):
        a_val, t_a, r_val, t_r, raw, u_full, v_full, pre, hidden = saved[step]
        if step < ITERS - 1:
            c_y, t_c_y = gather_tokens(token_block(c_state, t_c_state))
            part = jnp.concatenate([mdot(c_y, down), mdot(t_c_y, down) + mdot(c_y, dir_down)], axis=1)
            part, last_h = reduce_and_gather_z(reduce_x(part, x), last_hidden, z)
            c_h, t_c_h = halves(part)
            last_h = gather_x(last_h, x)
        c_pg, c_pu, t_c_pg, t_c_pu = hidden_backward(*pre, c_h[:, :HID], t_c_h[:, :HID])
        v_c = (r_val * c_pg, r_val * c_pu)
        u_c = (t_r * c_pg + r_val * t_c_pg, t_r * c_pu + r_val * t_c_pu)
        spare = ()
        if step > 0:
            u_g, u_u, v_g, v_u = raw
            spare = (
                row_sum(v_c[0] * u_g + v_c[1] * u_u),
                row_sum(v_c[0] * v_g + v_c[1] * v_u + u_c[0] * u_g + u_c[1] * u_u),
                r_val * r_val,
                r_val * t_r,
            )
        if step > 0:
            (c_v,) = gather_z(joined(*v_c, spare), z, (2 * SPAN,))
            (c_u,) = gather_z(joined(*u_c), z, (2 * SPAN,))
        else:
            both = jnp.concatenate([joined(*v_c), joined(*u_c)], axis=1)
            c_v, c_u = gather_z(both, z, (2 * SPAN, 2 * SPAN))
            c_v = after(c_v, last_h)
        c_v = gather_x(c_v, x)
        c_u = gather_x(c_u, x)
        if step == 0:
            late = after(last_h, c_u)
            acc_down = acc_down + inner_rows(last_c_y[0], late[:, SPAN:]) + inner_rows(last_c_y[1], late[:, :SPAN])
            acc_down = acc_down + inner_rows(c_y, hidden[1]) + inner_rows(t_c_y, hidden[0])
            u_full = after(u_full, acc_down)
        acc = acc + inner_rows(v_full, c_v) + inner_rows(u_full, c_u)
        if step > 0:
            q_val, t_q, sums = reduce_features(
                inner_cols(c_v, weights), inner_cols(c_u, weights) + inner_cols(c_v, dirs)
            )
            last_hidden = hidden
            last_c_y = (c_y, t_c_y)
            q_val = gain * q_val
            t_q = gain * t_q
            s_val, s_tan, r_sq, r_t_r = (sums[:, k : k + 1] + sums[:, k + 1 : k + 2] for k in (0, 2, 4, 6))
            r_sq = r_sq / 16
            r_t_r = r_t_r / 16
            beta = r_sq * s_val / D
            alpha = (2.0 * r_t_r * s_val + r_sq * s_tan) / D
            c_state = c_state + q_val - beta * a_val
            t_c_state = t_c_state + t_q - alpha * a_val - beta * t_a
    gate_est = (2 * gate_sign - 1).astype(F32) * acc[:FEAT, :HID]
    up_est = (2 * up_sign - 1).astype(F32) * acc[:FEAT, SPAN : SPAN + HID]
    down_est = (2 * down_sign - 1).astype(F32) * acc_down[:FEAT, :HID].T
    return (gate_est, up_est, down_est)


def solution(mesh):
    return jax.shard_map(
        per_device,
        mesh=mesh,
        in_specs=(
            P("row", "col"),
            P("row", "col"),
            P("row", "col"),
            P("col"),
            P("col", "row"),
            P("col", "row"),
            P("row", "col"),
            P("col", "row"),
            P("col", "row"),
            P("row", "col"),
        ),
        out_specs=(P("col", "row"), P("col", "row"), P("row", "col")),
        check_vma=False,
    )
```

```python
import jax
import jax.numpy as jnp
from jax import lax
from jax.sharding import PartitionSpec as P

D = 5280
FF = 17920
ITERS = 2
EPS = 1e-06

FEAT = 330
WIDE = 384
HID = 1120
SPAN = 1152
BF = jnp.bfloat16
F32 = jnp.float32

AT_X = [[(z * 4 + x, z * 4 + (x + k) % 4) for z in range(4) for x in range(4)] for k in range(4)]
AT_Z = [[(z * 4 + x, (z + k) % 4 * 4 + x) for z in range(4) for x in range(4)] for k in range(4)]
OTHER_CORE = [(i, i ^ 1) for i in range(16)]
OTHER_Z = [(i, i ^ 8) for i in range(16)]
AT_Y = [[(i, i // 8 * 8 + (i + 2 * k) % 8) for i in range(16)] for k in range(4)]


def mdot(left, right):
    return jnp.dot(left, right, preferred_element_type=F32)


def inner_rows(left, right):
    return lax.dot_general(left, right, (((0,), (0,)), ((), ())), preferred_element_type=F32)


def inner_cols(left, right):
    return lax.dot_general(left, right, (((1,), (1,)), ((), ())), preferred_element_type=F32)


def direction(sign, fan_in):
    return ((2 * sign - 1).astype(F32) * float(fan_in) ** (-0.5)).astype(BF)


def pad_to(array, rows, columns):
    return jnp.pad(array, ((0, rows - array.shape[0]), (0, columns - array.shape[1])))


def side_by_side(first, second):
    return jnp.concatenate([pad_to(first, WIDE, SPAN), pad_to(second, WIDE, SPAN)], axis=1)


def with_spare(array, wide, values):
    at = array.shape[1]
    array = pad_to(array, array.shape[0], wide)
    lane = lax.broadcasted_iota(jnp.int32, array.shape, 1)
    for value in values:
        high = lax.reduce_precision(value, 8, 7)
        array = jnp.where(lane == at, high, jnp.where(lane == at + 1, value - high, array))
        at += 2
    return array.astype(BF)


def exchange_sum(chunks, axis, place, perms):
    pieces = lax.optimization_barrier(
        tuple(lax.dynamic_index_in_dim(chunks, (place + k) % 4, axis, keepdims=False) for k in range(4))
    )
    got = lax.optimization_barrier(tuple(lax.ppermute(pieces[k], "col", perms[k]) for k in range(1, 4)))
    total = pieces[0].astype(F32)
    for piece in got:
        total = total + piece.astype(F32)
    return total


def reduce_x(partial, x):
    return exchange_sum(partial.astype(BF).reshape(4, 4, 16, -1), 1, x, AT_X).astype(BF)


def reduce_z(partial, z):
    return exchange_sum(partial, 0, z, AT_Z)


def reduce_and_gather_z(partial, block, z):
    width = partial.shape[2]
    pieces = lax.optimization_barrier(
        tuple(
            jnp.concatenate([lax.dynamic_index_in_dim(partial, (z + k) % 4, 0, keepdims=False), block], axis=1)
            for k in range(4)
        )
    )
    got = lax.optimization_barrier(tuple(lax.ppermute(pieces[k], "col", AT_Z[k]) for k in range(1, 4)))
    total = pieces[0][:, :width].astype(F32)
    for piece in got:
        total = total + piece[:, :width].astype(F32)
    return total, place_all(block, tuple(piece[:, width:] for piece in got), z, 0)


def place_all(own, got, place, axis):
    shape = own.shape[:axis] + (4,) + own.shape[axis:]
    out = jnp.zeros(shape, own.dtype)
    for k, piece in enumerate((own,) + got):
        out = lax.dynamic_update_slice_in_dim(out, jnp.expand_dims(piece, axis), (place - k) % 4, axis)
    return out


def gather_z(block, z, widths):
    got = lax.optimization_barrier(tuple(lax.ppermute(block, "col", AT_Z[k]) for k in range(1, 4)))
    outs, low = [], 0
    for width in widths:
        outs.append(place_all(block[:, low : low + width], tuple(g[:, low : low + width] for g in got), z, 0))
        low += width
    return outs


def gather_x(block, x):
    got = lax.optimization_barrier(tuple(lax.ppermute(block, "col", AT_X[k]) for k in range(1, 4)))
    return place_all(block, got, x, 1).reshape(256, -1)


def after(array, other):
    return array + (0.0 * other.reshape(-1, other.shape[-1])[:1, :1].astype(F32)).astype(array.dtype)


def halve(array, axis, bit, perm):
    keep = lax.dynamic_index_in_dim(array, bit, axis, keepdims=False)
    send = lax.dynamic_index_in_dim(array, 1 - bit, axis, keepdims=False)
    return (keep.astype(F32) + lax.ppermute(send, "row", perm).astype(F32)).astype(BF)


def row_place():
    place = lax.axis_index("row")
    return place // 8, place // 2 % 4, place % 2


def reduce_features(first, second):
    z, _, core = row_place()
    partial = jnp.concatenate([first, second], axis=1).astype(BF).reshape(2, 4, 2, 16, 2 * WIDE)
    partial = halve(partial, 2, core, OTHER_CORE)
    partial = halve(partial, 0, z, OTHER_Z)
    got = lax.optimization_barrier(tuple(lax.ppermute(partial, "row", AT_Y[k]) for k in range(1, 4)))
    total = partial.astype(F32)
    for piece in got:
        total = total + piece.astype(F32)
    total = total.reshape(64, 2 * WIDE)
    return total[:, :FEAT], total[:, WIDE : WIDE + FEAT], total[:, FEAT : FEAT + 8]


def token_block(first, second, stats=()):
    return jnp.concatenate([with_spare(first, WIDE, stats), with_spare(second, WIDE, ())], axis=1)


def gather_y(block):
    got = lax.optimization_barrier(tuple(lax.ppermute(block, "row", AT_Y[k]) for k in range(1, 4)))
    return place_all(block, got, row_place()[1], 0).reshape(64, -1)


def twice(block, axis, bit, perm):
    got = lax.ppermute(block, "row", perm)
    return jnp.where(bit == 0, jnp.stack([block, got], axis), jnp.stack([got, block], axis))


def gather_tokens(block):
    z, _, core = row_place()
    block = twice(block.reshape(4, 16, -1), 0, z, OTHER_Z)
    full = twice(block, 2, core, OTHER_CORE).reshape(256, -1)
    return tuple(full[:, at : at + WIDE] for at in range(0, full.shape[1], WIDE))


def halves(array):
    return array[:, :HID], array[:, SPAN : SPAN + HID]


def joined(first, second, spare=()):
    return jnp.concatenate([with_spare(first, SPAN, ()), with_spare(second, SPAN, spare)], axis=1)


def hidden_forward(pg, pu, t_pg, t_pu):
    sg = jax.nn.sigmoid(pg)
    act = pg * sg
    slope = sg * (1.0 + pg * (1.0 - sg))
    return act * pu, slope * t_pg * pu + act * t_pu


def hidden_backward(pg, pu, t_pg, t_pu, c_h, t_c_h):
    sg = jax.nn.sigmoid(pg)
    act = pg * sg
    slope = sg * (1.0 + pg * (1.0 - sg))
    curve = sg * (1.0 - sg) * (2.0 + pg * (1.0 - 2.0 * sg))
    c_pg = c_h * pu * slope
    c_pu = c_h * act
    t_c_pg = t_c_h * pu * slope + c_h * t_pu * slope + c_h * pu * curve * t_pg
    t_c_pu = t_c_h * act + c_h * slope * t_pg
    return c_pg, c_pu, t_c_pg, t_c_pu


def row_sum(array):
    return jnp.sum(array, axis=-1, keepdims=True)


def per_device(
    latent,
    embedded,
    cotangent,
    gain,
    gate_weight,
    up_weight,
    down_weight,
    gate_sign,
    up_sign,
    down_sign,
):
    place = lax.axis_index("col")
    x = place % 4
    z = place // 4
    weights = side_by_side(gate_weight, up_weight)
    row = lax.broadcasted_iota(jnp.int32, (WIDE, 2 * SPAN), 0) - FEAT
    column = lax.broadcasted_iota(jnp.int32, (WIDE, 2 * SPAN), 1)
    onward = (row >= 0) & (row < 4) & (column - HID - 4 * x == row)
    back = (row >= 0) & (row < 8) & (column - SPAN - HID == row)
    weights = jnp.where(onward | back, jnp.ones((), BF), weights)
    dirs = side_by_side(direction(gate_sign, D), direction(up_sign, D))
    down = pad_to(down_weight.T, WIDE, SPAN)
    dir_down = pad_to(direction(down_sign.T, FF), WIDE, SPAN)

    own = jnp.concatenate([pad_to(latent + embedded, 16, WIDE), pad_to(cotangent, 16, WIDE)], axis=1)
    own = gather_y(own)
    a_val = own[:, :FEAT]
    c_state = own[:, WIDE : WIDE + FEAT]
    t_a = jnp.zeros_like(a_val)
    t_c_state = jnp.zeros_like(c_state)
    saved = []
    for step in range(ITERS):
        stats = (row_sum(a_val * a_val), row_sum(a_val * t_a))
        block = token_block(a_val * gain, t_a * gain, stats)
        if step == 0:
            u_full, v_full, c_y, t_c_y = gather_tokens(
                jnp.concatenate([block, token_block(c_state, t_c_state)], axis=1)
            )
        else:
            u_full, v_full = gather_tokens(block)
            v_full = after(v_full, back)
        first = reduce_x(mdot(u_full, weights), x)
        second = reduce_x(mdot(v_full, weights) + mdot(u_full, dirs), x)
        if step > 0:
            first = jnp.concatenate([first, back[:, :, :SPAN]], axis=2)
            second = jnp.concatenate([second, back[:, :, SPAN:]], axis=2)
        first = reduce_z(first, z)
        second = reduce_z(second, z)
        if step == 0:
            aside = jnp.concatenate([mdot(c_y, down), mdot(t_c_y, down) + mdot(c_y, dir_down)], axis=1).astype(BF)
        else:
            c_h, t_c_h = first[:, 2 * SPAN :], second[:, 2 * SPAN :]
        spare = first[:, HID:SPAN]
        column = lax.broadcasted_iota(jnp.int32, spare.shape, 1)
        sum_sq = row_sum(jnp.where((column < 16) & (column % 4 < 2), spare, 0.0))
        sum_tan = row_sum(jnp.where((column < 16) & (column % 4 >= 2), spare, 0.0))
        r_val = lax.rsqrt(sum_sq / D + EPS)
        t_r = -0.5 * r_val * r_val * r_val * (2.0 * sum_tan / D)
        u_g, u_u = halves(first)
        v_g, v_u = halves(second)
        pre = (r_val * u_g, r_val * u_u, r_val * v_g + t_r * u_g, r_val * v_u + t_r * u_u)
        h_val, t_h = hidden_forward(*pre)
        hidden = joined(h_val, t_h)
        if step < ITERS - 1:
            (part,) = gather_z(hidden, z, (2 * SPAN,))
            full = gather_x(part, x)
            h_full, t_h_full = full[:, :SPAN], full[:, SPAN:]
            back = reduce_x(after(aside, full), x)
            y_val, t_y, _ = reduce_features(
                inner_cols(h_full, down), inner_cols(t_h_full, down) + inner_cols(h_full, dir_down)
            )
            hidden = (h_full, t_h_full)
        saved.append((a_val, t_a, r_val, t_r, (u_g, u_u, v_g, v_u), u_full, v_full, pre, hidden))
        if step < ITERS - 1:
            a_val = a_val + y_val
            t_a = t_a + t_y
    acc = jnp.zeros((WIDE, 2 * SPAN), F32)
    acc_down = jnp.zeros((WIDE, SPAN), F32)
    for step in reversed(range(ITERS)):
        a_val, t_a, r_val, t_r, raw, u_full, v_full, pre, hidden = saved[step]
        if step < ITERS - 1:
            c_y, t_c_y = gather_tokens(token_block(c_state, t_c_state))
            part = jnp.concatenate([mdot(c_y, down), mdot(t_c_y, down) + mdot(c_y, dir_down)], axis=1)
            part, last_h = reduce_and_gather_z(reduce_x(part, x), last_hidden, z)
            c_h, t_c_h = halves(part)
            last_h = gather_x(last_h, x)
        c_pg, c_pu, t_c_pg, t_c_pu = hidden_backward(*pre, c_h[:, :HID], t_c_h[:, :HID])
        v_c = (r_val * c_pg, r_val * c_pu)
        u_c = (t_r * c_pg + r_val * t_c_pg, t_r * c_pu + r_val * t_c_pu)
        spare = ()
        if step > 0:
            u_g, u_u, v_g, v_u = raw
            spare = (
                row_sum(v_c[0] * u_g + v_c[1] * u_u),
                row_sum(v_c[0] * v_g + v_c[1] * v_u + u_c[0] * u_g + u_c[1] * u_u),
                r_val * r_val,
                r_val * t_r,
            )
        if step > 0:
            (c_v,) = gather_z(joined(*v_c, spare), z, (2 * SPAN,))
            (c_u,) = gather_z(joined(*u_c), z, (2 * SPAN,))
        else:
            both = jnp.concatenate([joined(*v_c), joined(*u_c)], axis=1)
            c_v, c_u = gather_z(both, z, (2 * SPAN, 2 * SPAN))
            c_v = after(c_v, last_h)
        c_v = gather_x(c_v, x)
        c_u = gather_x(c_u, x)
        if step == 0:
            late = after(last_h, c_u)
            acc_down = acc_down + inner_rows(last_c_y[0], late[:, SPAN:]) + inner_rows(last_c_y[1], late[:, :SPAN])
            acc_down = acc_down + inner_rows(c_y, hidden[1]) + inner_rows(t_c_y, hidden[0])
            u_full = after(u_full, acc_down)
        acc = acc + inner_rows(v_full, c_v) + inner_rows(u_full, c_u)
        if step > 0:
            q_val, t_q, sums = reduce_features(
                inner_cols(c_v, weights), inner_cols(c_u, weights) + inner_cols(c_v, dirs)
            )
            last_hidden = hidden
            last_c_y = (c_y, t_c_y)
            q_val = gain * q_val
            t_q = gain * t_q
            s_val, s_tan, r_sq, r_t_r = (sums[:, k : k + 1] + sums[:, k + 1 : k + 2] for k in (0, 2, 4, 6))
            r_sq = r_sq / 16
            r_t_r = r_t_r / 16
            beta = r_sq * s_val / D
            alpha = (2.0 * r_t_r * s_val + r_sq * s_tan) / D
            c_state = c_state + q_val - beta * a_val
            t_c_state = t_c_state + t_q - alpha * a_val - beta * t_a
    gate_est = (2 * gate_sign - 1).astype(F32) * acc[:FEAT, :HID]
    up_est = (2 * up_sign - 1).astype(F32) * acc[:FEAT, SPAN : SPAN + HID]
    down_est = (2 * down_sign - 1).astype(F32) * acc_down[:FEAT, :HID].T
    return (gate_est, up_est, down_est)


def solution(mesh):
    return jax.shard_map(
        per_device,
        mesh=mesh,
        in_specs=(
            P("row", "col"),
            P("row", "col"),
            P("row", "col"),
            P("col"),
            P("col", "row"),
            P("col", "row"),
            P("row", "col"),
            P("col", "row"),
            P("col", "row"),
            P("row", "col"),
        ),
        out_specs=(P("col", "row"), P("col", "row"), P("row", "col")),
        check_vma=False,
    )
```
